32 devices in a mesh: sky: 8 (over z, x), vel: 4 (over y, core).
Axes of the slice: x: 2, y: 2, z: 4, core: 2. Of those that a mesh axis runs over, the one named last changes fastest.
Arguments:
- psi: float32 [4, 1024, 2048], P(None, 'sky', 'vel'), may hold values from -6 to 6
- phi: float32 [4, 1024, 2048], P(None, 'sky', 'vel'), may hold values from 0.25 to 4
- mask: int32 [4, 1024, 2048], P(None, 'sky', 'vel'), may hold values 0 or 1
- velocities: int32 [32, 2], replicated, may hold values from -12 to 12, as said below
- time_offsets: int32 [4], replicated, may hold values from 0 to 8, as said below
Outputs:
- likelihood: float32 [32, 1024, 2048], P('vel', 'sky')
The draws below stay inside these ranges and needn't reach their ends.
Inputs may be any that keep to these rules, and one draw needn't show every extreme that they name: `velocities`: every component lies in -12 .. 12. `time_offsets`: the first exposure's offset is 0.
All inputs are finite; a program needn't handle non-finite values. No bound on the sum of `mask` on one device may be relied on, other than what follows from the above.
Results may differ from the reference program's by a relative error of at most 0.0003.
Values sent between devices are 32-bit elements; how exact they have to be, the bound alone decides.
A program may use at most 128 MiB of HBM per device.

```python
import math
import jax
import jax.numpy as jnp
from jax import lax

E = 4
W = 2048
QMAX = 12
TMAX = 8
HALO = 25
NV = 32
H = 1024


def draw_velocities(key, part):
    values = jax.random.randint(jax.random.fold_in(key, 11), (NV, 2), -QMAX, QMAX + 1)
    first = jax.random.randint(jax.random.fold_in(key, 12), (), 0, NV)
    second = jax.random.randint(jax.random.fold_in(key, 13), (), 0, NV)
    values = values.at[first, 0].set(QMAX)
    values = values.at[second, 1].set(-QMAX)
    return values.astype(jnp.int32)


def draw_time_offsets(key, part):
    values = jax.random.randint(jax.random.fold_in(key, 21), (E,), 1, TMAX + 1)
    where_most = jax.random.randint(jax.random.fold_in(key, 22), (), 1, E)
    values = values.at[where_most].set(TMAX)
    values = values.at[0].set(0)
    return values.astype(jnp.int32)


def with_ends(values, rng, smallest, top_value):
    extent = values.shape
    place = [jax.random.randint(jax.random.fold_in(rng, axis), (), 0, extent[axis]) for axis in range(len(extent))]
    values = values.at[tuple(place)].set(smallest)
    longest = extent.index(max(extent))
    place[longest] = (place[longest] + 1) % extent[longest]
    return values.at[tuple(place)].set(top_value)


def shard_levels(key, extent, pieces, smallest, top_value):
    def one(dim, parts):
        steps = jax.random.uniform(jax.random.fold_in(jax.random.fold_in(key, 6), dim), (parts,), jnp.float32, smallest / len(pieces), top_value / len(pieces))
        return jnp.repeat(jnp.exp(steps), extent[dim] // parts).reshape((-1,) + (1,) * (len(extent) - dim - 1))

    level = one(*pieces[0])
    for cut in pieces[1:]:
        level = level * one(*cut)
    return level


def scatter_about(key, dims, scale, reach, pieces=(), held_as=jnp.bfloat16):
    loudness = shard_levels(key, dims, pieces, -0.22, 0.18) if pieces else 1.0
    drawn = jax.random.normal(key, dims, jnp.float32) * scale * loudness
    return jnp.minimum(jnp.maximum(drawn, -reach), reach).astype(held_as)


def setup_inputs(seed: int = 0) -> dict:
    key_of = jax.random.split(jax.random.key(seed), 6)
    return {
        "psi": scatter_about(key_of[0], (E, H, W), 1.0, 6.0, ((1, 8), (2, 4)), jnp.float32),
        "phi": jnp.clip(jnp.exp(math.log(4.0) - 2.7725887 * jax.random.uniform(key_of[1], (E, H, W), jnp.float32) ** shard_levels(key_of[1], (E, H, W), ((1, 8), (2, 4)), -0.2, 0.2)), 0.25, 4.0),
        "mask": with_ends((jax.random.randint(key_of[2], (E, H, W), 0, 8) < 1).astype(jnp.int32), jax.random.fold_in(key_of[2], 1), 0, 1),
        "velocities": draw_velocities(jax.random.fold_in(key_of[5], 71), 0),
        "time_offsets": draw_time_offsets(jax.random.fold_in(key_of[5], 71), 0),
    }


def stack_maps(padded, velocity, time_offsets, rows, cols):
    total = jnp.zeros((2, rows, cols), jnp.float32)
    for exposure in range(padded.shape[1]):
        shift_row = velocity[0] * time_offsets[exposure]
        shift_col = velocity[1] * time_offsets[exposure]
        whole_row = jnp.floor_divide(shift_row, 4)
        whole_col = jnp.floor_divide(shift_col, 4)
        frac_row = (shift_row - 4 * whole_row).astype(jnp.float32) * 0.25
        frac_col = (shift_col - 4 * whole_col).astype(jnp.float32) * 0.25
        window = lax.dynamic_slice(padded[:, exposure], (jnp.int32(0), (HALO + whole_row).astype(jnp.int32), (HALO + whole_col).astype(jnp.int32)), (2, rows + 1, cols + 1))
        upper = (1.0 - frac_col) * window[:, :-1, :-1] + frac_col * window[:, :-1, 1:]
        lower = (1.0 - frac_col) * window[:, 1:, :-1] + frac_col * window[:, 1:, 1:]
        total = total + ((1.0 - frac_row) * upper + frac_row * lower)
    return total[0] / jnp.sqrt(jnp.maximum(total[1], 1.0))

def reference(psi, phi, mask, velocities, time_offsets):
    keep = mask == 0
    stacked = jnp.stack([jnp.where(keep, psi, 0.0), jnp.where(keep, phi, 0.0)])
    padded = jnp.pad(stacked, ((0, 0), (0, 0), (HALO, HALO), (HALO, HALO)))
    rows = psi.shape[1]
    cols = psi.shape[2]

    def one_velocity(velocity):
        return stack_maps(padded, velocity, time_offsets, rows, cols)
    return lax.map(one_velocity, velocities)
```

```python
import functools

import jax
import jax.numpy as jnp
from jax import lax
from jax.experimental import pallas as pl
from jax.experimental.pallas import tpu as pltpu
from jax.sharding import PartitionSpec as P

REACH = 24
LANES = 128
MIB = 1024 * 1024


def keep_kernel(psi_ref, phi_ref, mask_ref, edges_ref, mid_ref, first_ref):
    exposures, rows, cols = psi_ref.shape
    for exposure in range(exposures):
        for tile in range(cols // LANES):
            columns = pl.ds(tile * LANES, LANES)
            keep = mask_ref[exposure, :, columns] == 0
            for layer, ref in enumerate((psi_ref, phi_ref)):
                kept = jnp.where(keep, ref[exposure, :, columns], 0.0)
                if exposure == 0:
                    first_ref[layer, tile] = kept
                else:
                    edges_ref[0, exposure - 1, layer, tile] = kept[:REACH]
                    mid_ref[exposure - 1, layer, tile] = kept[REACH : rows - REACH]
                    edges_ref[1, exposure - 1, layer, tile] = kept[rows - REACH :]


def keep(psi, phi, mask):
    exposures, rows, cols = psi.shape
    tiles = cols // LANES
    later = exposures - 1
    f32 = jnp.float32
    return pl.pallas_call(
        keep_kernel,
        out_shape=(
            jax.ShapeDtypeStruct((2, later, 2, tiles, REACH, LANES), f32),
            jax.ShapeDtypeStruct((later, 2, tiles, rows - 2 * REACH, LANES), f32),
            jax.ShapeDtypeStruct((2, tiles, rows, LANES), f32),
        ),
        compiler_params=pltpu.CompilerParams(vmem_limit_bytes=32 * MIB),
    )(psi, phi, mask)


def stack_kernel(pieces, tiles, later, rows, per_device, *refs):
    velocity_ref, offset_ref, owner_ref = refs[:3]
    piece_refs = refs[3 : 3 + 5 * pieces]
    out_ref, image, first, sems = refs[3 + 5 * pieces :]
    all_tiles = pieces * tiles
    step = pl.program_id(0)
    lane = lax.broadcasted_iota(jnp.int32, (8, LANES), 1)

    @pl.when(step == 0)
    def _():
        copies = []
        for piece in range(pieces):
            above, edges, mid, below, own_first = piece_refs[5 * piece : 5 * piece + 5]
            place = owner_ref[piece] * tiles
            moves = (
                (above, 0, REACH),
                (edges.at[0], REACH, REACH),
                (mid, 2 * REACH, rows - 2 * REACH),
                (edges.at[1], rows, REACH),
                (below, rows + REACH, REACH),
            )
            for source, start, count in moves:
                target = image.at[:, :, 0, pl.ds(1 + place, tiles), pl.ds(start, count), :]
                copies.append(pltpu.make_async_copy(source, target, sems.at[len(copies)]))
            target = first.at[:, pl.ds(place, tiles)]
            copies.append(pltpu.make_async_copy(own_first, target, sems.at[len(copies)]))
        for copy in copies:
            copy.start()
        depth = image.shape[4]
        blank = jnp.zeros((depth, LANES), jnp.float32)
        for exposure in range(later):
            for layer in range(2):
                image[exposure, layer, 0, 0] = blank
                for part in range(4):
                    image[exposure, layer, part, all_tiles + 1] = blank
                for tile in range(all_tiles):
                    image[exposure, layer, 0, tile + 1, rows + 2 * REACH :] = blank[rows + 2 * REACH :]
        for copy in copies:
            copy.wait()
        wide_lane = lax.broadcasted_iota(jnp.int32, (depth, LANES), 1)

        def interpolate(index, carry):
            exposure = index // (2 * (all_tiles + 1))
            layer = index // (all_tiles + 1) % 2
            tile = index % (all_tiles + 1)
            left = image[exposure, layer, 0, tile]
            right = image[exposure, layer, 0, tile + 1]
            moved = jnp.where(
                wide_lane < LANES - 1,
                pltpu.roll(left, LANES - 1, 1),
                pltpu.roll(right, LANES - 1, 1),
            )
            slope = moved - left
            for part in range(1, 4):
                image[exposure, layer, part, tile] = left + (0.25 * part) * slope
            return carry

        lax.fori_loop(0, later * 2 * (all_tiles + 1), interpolate, 0)

    index = owner_ref[0] * per_device + step
    plans = []
    for exposure in range(later):
        row_shift = velocity_ref[index, 0] * offset_ref[exposure + 1]
        col_shift = velocity_ref[index, 1] * offset_ref[exposure + 1]
        frac_row = jnp.broadcast_to((row_shift & 3).astype(jnp.float32) * 0.25, (8, LANES))
        start = LANES + (col_shift >> 2)
        inside = start & (LANES - 1)
        plans.append(
            (
                REACH + (row_shift >> 2),
                frac_row,
                col_shift & 3,
                start >> 7,
                (LANES - inside) & (LANES - 1),
                lane < LANES - inside,
            )
        )

    def row_group(group, carry):
        def turned(exposure, layer, tile):
            base, frac_row, part, skip, turn, _ = plans[exposure]
            upper = image[exposure, layer, part, skip + tile, pl.ds(base + 8 * group, 8), :]
            lower = image[exposure, layer, part, skip + tile, pl.ds(base + 8 * group + 1, 8), :]
            return pltpu.roll(upper + frac_row * (lower - upper), turn, 1)

        lanes = [(e, l) for e in range(later) for l in range(2)]
        held = {key: turned(*key, 0) for key in lanes}
        for tile in range(all_tiles):
            total = [first[layer, tile, pl.ds(pl.multiple_of(8 * group, 8), 8), :] for layer in range(2)]
            for key in lanes:
                following = turned(*key, tile + 1)
                total[key[1]] += jnp.where(plans[key[0]][5], held[key], following)
                held[key] = following
            out_ref[0, group, tile] = total[0] * lax.rsqrt(jnp.maximum(total[1], 1.0))
        return carry

    lax.fori_loop(0, rows // 8, row_group, 0)


def stack(velocities, time_offsets, owners, pieces, per_device):
    count = len(pieces)
    later, _, tiles, _, _ = pieces[0][2].shape
    rows = pieces[0][4].shape[2]
    all_tiles = count * tiles
    depth = rows + 2 * REACH + 8
    smem = pl.BlockSpec(memory_space=pltpu.SMEM)
    anywhere = pl.BlockSpec(memory_space=pl.ANY)
    flat = [array for piece in pieces for array in piece]
    out = pl.pallas_call(
        functools.partial(stack_kernel, count, tiles, later, rows, per_device),
        grid=(per_device,),
        out_shape=jax.ShapeDtypeStruct((per_device, rows // 8, all_tiles, 8, LANES), jnp.float32),
        in_specs=[smem] * 3 + [anywhere] * len(flat),
        out_specs=pl.BlockSpec((1, rows // 8, all_tiles, 8, LANES), lambda v: (v, 0, 0, 0, 0)),
        scratch_shapes=[
            pltpu.VMEM((later, 2, 4, all_tiles + 2, depth, LANES), jnp.float32),
            pltpu.VMEM((2, all_tiles, rows, LANES), jnp.float32),
            pltpu.SemaphoreType.DMA((6 * count,)),
        ],
        compiler_params=pltpu.CompilerParams(vmem_limit_bytes=56 * MIB),
    )(velocities, time_offsets, owners, *flat)
    return out.transpose(0, 1, 3, 2, 4).reshape(per_device, rows, all_tiles * LANES)


def after(value, *earlier):
    return lax.optimization_barrier((value, *earlier))[0]


def body(psi, phi, mask, velocities, time_offsets):
    count = lax.axis_size("vel")
    skies = lax.axis_size("sky")
    per_device = velocities.shape[0] // count
    me = lax.axis_index("vel")
    edges, mid, first = keep(psi, phi, mask)

    def swap(value, bits):
        return lax.ppermute(value, "vel", [(i, i ^ bits) for i in range(count)])

    def from_rows_above(value):
        return lax.ppermute(value, "sky", [(i, i + 1) for i in range(skies - 1)])

    def from_rows_below(value):
        return lax.ppermute(value, "sky", [(i + 1, i) for i in range(skies - 1)])

    far = [2 * k for k in range(1, count // 2)]
    far_edges = [edges] + [swap(edges, bits) for bits in far]
    far_mid = [mid] + [swap(after(mid, far_edges[-1]), bits) for bits in far]
    far_first = [first] + [swap(after(first, far_mid[-1]), bits) for bits in far]
    pieces, owners = [], []
    for k in range(count // 2):
        above = from_rows_above(far_edges[k][1])
        below = from_rows_below(far_edges[k][0])
        pieces.append((above, far_edges[k], far_mid[k], below, far_first[k]))
        owners.append(me ^ (2 * k))
    for k in range(count // 2):
        pieces.append(tuple(swap(array, 1) for array in pieces[k]))
        owners.append(me ^ (2 * k + 1))
    owners = jnp.stack(owners).astype(jnp.int32)
    return stack(velocities, time_offsets, owners, pieces, per_device)


def solution(mesh):
    return jax.shard_map(
        body,
        mesh=mesh,
        in_specs=(P(None, "sky", "vel"), P(None, "sky", "vel"), P(None, "sky", "vel"), P(), P()),
        out_specs=P("vel", "sky", None),
        check_vma=False,
    )
```

```python
import functools

import jax
import jax.numpy as jnp
from jax import lax
from jax.experimental import pallas as pl
from jax.experimental.pallas import tpu as pltpu
from jax.sharding import PartitionSpec as P

REACH = 24
LANES = 128
MIB = 1024 * 1024


def keep_kernel(psi_ref, phi_ref, mask_ref, top_ref, bottom_ref, mid_ref, last_ref, first_ref):
    exposures, rows, cols = psi_ref.shape
    for exposure in range(exposures):
        for tile in range(cols // LANES):
            columns = pl.ds(tile * LANES, LANES)
            keep = mask_ref[exposure, :, columns] == 0
            for layer, ref in enumerate((psi_ref, phi_ref)):
                kept = jnp.where(keep, ref[exposure, :, columns], 0.0)
                if exposure == 0:
                    first_ref[layer, tile] = kept
                    continue
                top_ref[exposure - 1, layer, tile] = kept[:REACH]
                bottom_ref[exposure - 1, layer, tile] = kept[rows - REACH :]
                middle = kept[REACH : rows - REACH]
                if exposure == exposures - 1:
                    last_ref[0, layer, tile] = middle
                else:
                    mid_ref[exposure - 1, layer, tile] = middle


def keep(psi, phi, mask):
    exposures, rows, cols = psi.shape
    tiles = cols // LANES
    later = exposures - 1
    shapes = [(later, 2, tiles, REACH, LANES)] * 2 + [
        (later - 1, 2, tiles, rows - 2 * REACH, LANES),
        (1, 2, tiles, rows - 2 * REACH, LANES),
        (2, tiles, rows, LANES),
    ]
    return pl.pallas_call(
        keep_kernel,
        out_shape=tuple(jax.ShapeDtypeStruct(shape, jnp.float32) for shape in shapes),
        compiler_params=pltpu.CompilerParams(vmem_limit_bytes=32 * MIB),
    )(psi, phi, mask)


def stack_kernel(pieces, tiles, begin, later, rows, per_device, final, *refs):
    velocity_ref, offset_ref, owner_ref = refs[:3]
    each = 6 if final else 5
    piece_refs = refs[3 : 3 + each * pieces]
    rest = refs[3 + each * pieces :]
    if final:
        sum_ref, out_ref, image, sems, first = rest
    else:
        out_ref, image, sems = rest
    all_tiles = pieces * tiles
    step = pl.program_id(0)
    lane = lax.broadcasted_iota(jnp.int32, (8, LANES), 1)

    @pl.when(step == 0)
    def _():
        copies = []
        for piece in range(pieces):
            above, top, mid, bottom, below = piece_refs[each * piece : each * piece + 5]
            place = owner_ref[piece] * tiles
            mine = pl.ds(begin, later)
            moves = (
                (above.at[mine], 0, REACH),
                (top.at[mine], REACH, REACH),
                (mid, 2 * REACH, rows - 2 * REACH),
                (bottom.at[mine], rows, REACH),
                (below.at[mine], rows + REACH, REACH),
            )
            for source, start, count in moves:
                target = image.at[:, :, 0, pl.ds(1 + place, tiles), pl.ds(start, count), :]
                copies.append(pltpu.make_async_copy(source, target, sems.at[len(copies)]))
            if final:
                target = first.at[:, pl.ds(place, tiles)]
                source = piece_refs[each * piece + 5]
                copies.append(pltpu.make_async_copy(source, target, sems.at[len(copies)]))
        for copy in copies:
            copy.start()
        depth = image.shape[4]
        blank = jnp.zeros((depth, LANES), jnp.float32)
        for exposure in range(later):
            for layer in range(2):
                image[exposure, layer, 0, 0] = blank
                for part in range(4):
                    image[exposure, layer, part, all_tiles + 1] = blank
                for tile in range(all_tiles):
                    image[exposure, layer, 0, tile + 1, rows + 2 * REACH :] = blank[rows + 2 * REACH :]
        for copy in copies:
            copy.wait()
        groups = depth // 8

        def interpolate(index, carry):
            exposure = index // (2 * groups)
            layer = index // groups % 2
            here = pl.ds(pl.multiple_of(index % groups * 8, 8), 8)
            left = image[exposure, layer, 0, 0, here, :]
            left_moved = pltpu.roll(left, LANES - 1, 1)
            for tile in range(all_tiles + 1):
                right = image[exposure, layer, 0, tile + 1, here, :]
                right_moved = pltpu.roll(right, LANES - 1, 1)
                slope = jnp.where(lane < LANES - 1, left_moved, right_moved) - left
                for part in range(1, 4):
                    image[exposure, layer, part, tile, here, :] = left + (0.25 * part) * slope
                left, left_moved = right, right_moved
            return carry

        lax.fori_loop(0, later * 2 * groups, interpolate, 0)

    index = owner_ref[0] * per_device + step
    plans = []
    for exposure in range(later):
        offset = offset_ref[begin + exposure + 1]
        row_shift = velocity_ref[index, 0] * offset
        col_shift = velocity_ref[index, 1] * offset
        frac_row = jnp.broadcast_to((row_shift & 3).astype(jnp.float32) * 0.25, (8, LANES))
        start = LANES + (col_shift >> 2)
        inside = start & (LANES - 1)
        plans.append(
            (
                REACH + (row_shift >> 2),
                frac_row,
                col_shift & 3,
                start >> 7,
                (LANES - inside) & (LANES - 1),
                lane < LANES - inside,
            )
        )

    def row_group(group, carry):
        def turned(exposure, layer, tile):
            base, frac_row, part, skip, turn, _ = plans[exposure]
            upper = image[exposure, layer, part, skip + tile, pl.ds(base + 8 * group, 8), :]
            lower = image[exposure, layer, part, skip + tile, pl.ds(base + 8 * group + 1, 8), :]
            return pltpu.roll(upper + frac_row * (lower - upper), turn, 1)

        held = {(e, l): turned(e, l, 0) for e in range(later) for l in range(2)}
        here = pl.ds(pl.multiple_of(8 * group, 8), 8)
        for tile in range(all_tiles):
            total = []
            for layer in range(2):
                terms = []
                if final:
                    terms = [first[layer, tile, here, :], sum_ref[0, layer, group, tile]]
                for exposure in range(later):
                    following = turned(exposure, layer, tile + 1)
                    terms.append(jnp.where(plans[exposure][5], held[exposure, layer], following))
                    held[exposure, layer] = following
                total.append(functools.reduce(jnp.add, terms))
            if final:
                out_ref[0, group, tile] = total[0] * lax.rsqrt(jnp.maximum(total[1], 1.0))
            else:
                out_ref[0, 0, group, tile] = total[0]
                out_ref[0, 1, group, tile] = total[1]
        return carry

    lax.fori_loop(0, rows // 8, row_group, 0)


def stack(velocities, time_offsets, owners, pieces, begin, rows, per_device, sums=None):
    final = sums is not None
    count = len(pieces)
    later, _, tiles, _, _ = pieces[0][2].shape
    all_tiles = count * tiles
    depth = rows + 2 * REACH + 8
    smem = pl.BlockSpec(memory_space=pltpu.SMEM)
    anywhere = pl.BlockSpec(memory_space=pl.ANY)
    block = (rows // 8, all_tiles, 8, LANES)
    sum_shape = (per_device, 2) + block
    out_shape = (per_device,) + block if final else sum_shape
    sum_spec = pl.BlockSpec((1, 2) + block, lambda v: (v, 0, 0, 0, 0, 0))
    out_spec = pl.BlockSpec((1,) + block, lambda v: (v, 0, 0, 0, 0)) if final else sum_spec
    flat = [array for piece in pieces for array in piece]
    scratch = [
        pltpu.VMEM((later, 2, 4, all_tiles + 2, depth, LANES), jnp.float32),
        pltpu.SemaphoreType.DMA((6 * count,)),
    ]
    if final:
        scratch.append(pltpu.VMEM((2, all_tiles, rows, LANES), jnp.float32))
    return pl.pallas_call(
        functools.partial(stack_kernel, count, tiles, begin, later, rows, per_device, final),
        grid=(per_device,),
        out_shape=jax.ShapeDtypeStruct(out_shape, jnp.float32),
        in_specs=[smem] * 3 + [anywhere] * len(flat) + ([sum_spec] if final else []),
        out_specs=out_spec,
        scratch_shapes=scratch,
        compiler_params=pltpu.CompilerParams(vmem_limit_bytes=44 * MIB),
        cost_estimate=pl.CostEstimate(
            flops=later * 8_000_000_000, bytes_accessed=later * 16 * MIB, transcendentals=0
        ),
    )(velocities, time_offsets, owners, *flat, *([sums] if final else []))


def after(value, *earlier):
    return lax.optimization_barrier((value, *earlier))[0]


def body(psi, phi, mask, velocities, time_offsets):
    count = lax.axis_size("vel")
    skies = lax.axis_size("sky")
    rows = psi.shape[1]
    later = psi.shape[0] - 1
    per_device = velocities.shape[0] // count
    me = lax.axis_index("vel")
    top, bottom, mid, last, first = keep(psi, phi, mask)

    def swap(value, bits):
        return lax.ppermute(value, "vel", [(i, i ^ bits) for i in range(count)])

    def from_rows_above(value):
        return lax.ppermute(value, "sky", [(i, i + 1) for i in range(skies - 1)])

    def from_rows_below(value):
        return lax.ppermute(value, "sky", [(i + 1, i) for i in range(skies - 1)])

    far = [2 * k for k in range(1, count // 2)]

    def gathered(value, *earlier):
        return [value] + [swap(after(value, *earlier), bits) for bits in far]

    tops = gathered(top)
    bottoms = gathered(bottom)
    mids = gathered(mid, tops[-1], bottoms[-1])
    lasts = gathered(last, mids[-1])
    firsts = gathered(first, lasts[-1])
    aboves = [from_rows_above(value) for value in bottoms]
    belows = [from_rows_below(value) for value in tops]
    owners = [me ^ (2 * k) for k in range(count // 2)] + [me ^ (2 * k + 1) for k in range(count // 2)]
    owners = jnp.stack(owners).astype(jnp.int32)

    def both_cores(arrays):
        return arrays + [swap(value, 1) for value in arrays]

    aboves, tops, bottoms, belows = map(both_cores, (aboves, tops, bottoms, belows))
    pieces = list(zip(aboves, tops, both_cores(mids), bottoms, belows))
    sums = stack(velocities, time_offsets, owners, pieces, 0, rows, per_device)
    firsts = [first] + [after(value, sums) for value in firsts[1:]]
    pieces = list(zip(aboves, tops, both_cores(lasts), bottoms, belows, both_cores(firsts)))
    out = stack(velocities, time_offsets, owners, pieces, later - 1, rows, per_device, sums)
    return out.transpose(0, 1, 3, 2, 4).reshape(per_device, rows, -1)


def solution(mesh):
    return jax.shard_map(
        body,
        mesh=mesh,
        in_specs=(P(None, "sky", "vel"), P(None, "sky", "vel"), P(None, "sky", "vel"), P(), P()),
        out_specs=P("vel", "sky", None),
        check_vma=False,
    )
```

```python
import functools

import jax
import jax.numpy as jnp
from jax import lax
from jax.experimental import pallas as pl
from jax.experimental.pallas import tpu as pltpu
from jax.sharding import PartitionSpec as P

REACH = 24
LANES = 128
MIB = 1024 * 1024


def keep_kernel(psi_ref, phi_ref, mask_ref, edges_ref, mid_ref, first_ref):
    exposures, rows, cols = psi_ref.shape
    for exposure in range(exposures):
        for tile in range(cols // LANES):
            columns = pl.ds(tile * LANES, LANES)
            keep = mask_ref[exposure, :, columns] == 0
            for layer, ref in enumerate((psi_ref, phi_ref)):
                kept = jnp.where(keep, ref[exposure, :, columns], 0.0)
                if exposure == 0:
                    first_ref[layer, tile] = kept
                else:
                    edges_ref[0, exposure - 1, layer, tile] = kept[:REACH]
                    mid_ref[exposure - 1, layer, tile] = kept[REACH : rows - REACH]
                    edges_ref[1, exposure - 1, layer, tile] = kept[rows - REACH :]


def keep(psi, phi, mask):
    exposures, rows, cols = psi.shape
    tiles = cols // LANES
    later = exposures - 1
    f32 = jnp.float32
    return pl.pallas_call(
        keep_kernel,
        out_shape=(
            jax.ShapeDtypeStruct((2, later, 2, tiles, REACH, LANES), f32),
            jax.ShapeDtypeStruct((later, 2, tiles, rows - 2 * REACH, LANES), f32),
            jax.ShapeDtypeStruct((2, tiles, rows, LANES), f32),
        ),
        compiler_params=pltpu.CompilerParams(vmem_limit_bytes=32 * MIB),
    )(psi, phi, mask)


def stack_kernel(pieces, tiles, later, rows, per_device, *refs):
    velocity_ref, offset_ref, owner_ref = refs[:3]
    piece_refs = refs[3 : 3 + 5 * pieces]
    out_ref, image, first, sems = refs[3 + 5 * pieces :]
    all_tiles = pieces * tiles
    step = pl.program_id(0)
    lane = lax.broadcasted_iota(jnp.int32, (8, LANES), 1)

    @pl.when(step == 0)
    def _():
        waves = [[] for _ in range(later + 1)]
        started = 0
        for exposure in range(later):
            for piece in range(pieces):
                above, edges, mid, below, _ = piece_refs[5 * piece : 5 * piece + 5]
                place = owner_ref[piece] * tiles
                moves = (
                    (above.at[exposure], 0, REACH),
                    (edges.at[0, exposure], REACH, REACH),
                    (mid.at[exposure], 2 * REACH, rows - 2 * REACH),
                    (edges.at[1, exposure], rows, REACH),
                    (below.at[exposure], rows + REACH, REACH),
                )
                for source, start, count in moves:
                    target = image.at[exposure, :, 0, pl.ds(1 + place, tiles), pl.ds(start, count), :]
                    waves[exposure].append(pltpu.make_async_copy(source, target, sems.at[started]))
                    started += 1
        for piece in range(pieces):
            target = first.at[:, pl.ds(owner_ref[piece] * tiles, tiles)]
            source = piece_refs[5 * piece + 4]
            waves[later].append(pltpu.make_async_copy(source, target, sems.at[started]))
            started += 1
        for wave in waves:
            for copy in wave:
                copy.start()
        depth = image.shape[4]
        blank = jnp.zeros((depth, LANES), jnp.float32)
        for exposure in range(later):
            for layer in range(2):
                image[exposure, layer, 0, 0] = blank
                for part in range(4):
                    image[exposure, layer, part, all_tiles + 1] = blank
                for tile in range(all_tiles):
                    image[exposure, layer, 0, tile + 1, rows + 2 * REACH :] = blank[rows + 2 * REACH :]
        groups = depth // 8

        def interpolate(exposure, index, carry):
            layer = index // groups
            here = pl.ds(pl.multiple_of(index % groups * 8, 8), 8)
            values = [image[exposure, layer, 0, tile, here, :] for tile in range(all_tiles + 2)]
            moved = [pltpu.roll(value, LANES - 1, 1) for value in values]
            for tile in range(all_tiles + 1):
                slope = jnp.where(lane < LANES - 1, moved[tile], moved[tile + 1]) - values[tile]
                for part in range(1, 4):
                    image[exposure, layer, part, tile, here, :] = values[tile] + (0.25 * part) * slope
            return carry

        for exposure in range(later):
            for copy in waves[exposure]:
                copy.wait()
            lax.fori_loop(0, 2 * groups, functools.partial(interpolate, exposure), 0)
        for copy in waves[later]:
            copy.wait()

    index = owner_ref[0] * per_device + step
    plans = []
    for exposure in range(later):
        row_shift = velocity_ref[index, 0] * offset_ref[exposure + 1]
        col_shift = velocity_ref[index, 1] * offset_ref[exposure + 1]
        frac_row = jnp.broadcast_to((row_shift & 3).astype(jnp.float32) * 0.25, (8, LANES))
        start = LANES + (col_shift >> 2)
        inside = start & (LANES - 1)
        plans.append(
            (
                REACH + (row_shift >> 2),
                frac_row,
                col_shift & 3,
                start >> 7,
                (LANES - inside) & (LANES - 1),
                lane < LANES - inside,
            )
        )

    def row_group(group, carry):
        def turned(exposure, layer, tile):
            base, frac_row, part, skip, turn, _ = plans[exposure]
            upper = image[exposure, layer, part, skip + tile, pl.ds(base + 8 * group, 8), :]
            lower = image[exposure, layer, part, skip + tile, pl.ds(base + 8 * group + 1, 8), :]
            return pltpu.roll(upper + frac_row * (lower - upper), turn, 1)

        lanes = [(e, l) for e in range(later) for l in range(2)]
        held = {key: turned(*key, 0) for key in lanes}
        done = []
        for tile in range(all_tiles):
            total = [first[layer, tile, pl.ds(pl.multiple_of(8 * group, 8), 8), :] for layer in range(2)]
            for key in lanes:
                following = turned(*key, tile + 1)
                total[key[1]] += jnp.where(plans[key[0]][5], held[key], following)
                held[key] = following
            done.append(total[0] * lax.rsqrt(jnp.maximum(total[1], 1.0)))
        for tile in range(all_tiles):
            out_ref[0, group, tile] = done[tile]
        return carry

    lax.fori_loop(0, rows // 8, row_group, 0)


def stack(velocities, time_offsets, owners, pieces, per_device):
    count = len(pieces)
    later, _, tiles, _, _ = pieces[0][2].shape
    rows = pieces[0][4].shape[2]
    all_tiles = count * tiles
    depth = rows + 2 * REACH + 8
    smem = pl.BlockSpec(memory_space=pltpu.SMEM)
    anywhere = pl.BlockSpec(memory_space=pl.ANY)
    flat = [array for piece in pieces for array in piece]
    out = pl.pallas_call(
        functools.partial(stack_kernel, count, tiles, later, rows, per_device),
        grid=(per_device,),
        out_shape=jax.ShapeDtypeStruct((per_device, rows // 8, all_tiles, 8, LANES), jnp.float32),
        in_specs=[smem] * 3 + [anywhere] * len(flat),
        out_specs=pl.BlockSpec((1, rows // 8, all_tiles, 8, LANES), lambda v: (v, 0, 0, 0, 0)),
        scratch_shapes=[
            pltpu.VMEM((later, 2, 4, all_tiles + 2, depth, LANES), jnp.float32),
            pltpu.VMEM((2, all_tiles, rows, LANES), jnp.float32),
            pltpu.SemaphoreType.DMA(((5 * later + 1) * count,)),
        ],
        compiler_params=pltpu.CompilerParams(vmem_limit_bytes=56 * MIB),
    )(velocities, time_offsets, owners, *flat)
    return out.transpose(0, 1, 3, 2, 4).reshape(per_device, rows, all_tiles * LANES)


def after(value, *earlier):
    return lax.optimization_barrier((value, *earlier))[0]


def body(psi, phi, mask, velocities, time_offsets):
    count = lax.axis_size("vel")
    skies = lax.axis_size("sky")
    per_device = velocities.shape[0] // count
    me = lax.axis_index("vel")
    edges, mid, first = keep(psi, phi, mask)

    def swap(value, bits):
        return lax.ppermute(value, "vel", [(i, i ^ bits) for i in range(count)])

    def from_rows_above(value):
        return lax.ppermute(value, "sky", [(i, i + 1) for i in range(skies - 1)])

    def from_rows_below(value):
        return lax.ppermute(value, "sky", [(i + 1, i) for i in range(skies - 1)])

    far = [2 * k for k in range(1, count // 2)]
    above, below = from_rows_above(edges[1]), from_rows_below(edges[0])
    far_edges = [edges] + [swap(edges, bits) for bits in far]
    sent = after(mid, far_edges[-1], above, below)
    far_mid = [mid] + [swap(sent, bits) for bits in far]
    above, below = [above], [below]
    for value in far_edges[1:]:
        above.append(from_rows_above(value[1]))
        below.append(from_rows_below(value[0]))
    sent = after(first, far_mid[-1], above[-1], below[-1])
    far_first = [first] + [swap(sent, bits) for bits in far]
    pieces, owners = [], []
    for k in range(count // 2):
        pieces.append((above[k], far_edges[k], far_mid[k], below[k], far_first[k]))
        owners.append(me ^ (2 * k))
    for k in range(count // 2):
        pieces.append(tuple(swap(array, 1) for array in pieces[k]))
        owners.append(me ^ (2 * k + 1))
    owners = jnp.stack(owners).astype(jnp.int32)
    return stack(velocities, time_offsets, owners, pieces, per_device)


def solution(mesh):
    return jax.shard_map(
        body,
        mesh=mesh,
        in_specs=(P(None, "sky", "vel"), P(None, "sky", "vel"), P(None, "sky", "vel"), P(), P()),
        out_specs=P("vel", "sky", None),
        check_vma=False,
    )
```

```python
import functools

import jax
import jax.numpy as jnp
from jax import lax
from jax.experimental import pallas as pl
from jax.experimental.pallas import tpu as pltpu
from jax.sharding import PartitionSpec as P

REACH = 24
LANES = 128
MIB = 1024 * 1024


def keep_kernel(psi_ref, phi_ref, mask_ref, edges_ref, mid_ref, first_ref):
    exposures, rows, cols = psi_ref.shape
    for exposure in range(exposures):
        for tile in range(cols // LANES):
            columns = pl.ds(tile * LANES, LANES)
            keep = mask_ref[exposure, :, columns] == 0
            for layer, ref in enumerate((psi_ref, phi_ref)):
                kept = jnp.where(keep, ref[exposure, :, columns], 0.0)
                if exposure == 0:
                    first_ref[layer, tile] = kept
                else:
                    edges_ref[0, exposure - 1, layer, tile] = kept[:REACH]
                    mid_ref[exposure - 1, layer, tile] = kept[REACH : rows - REACH]
                    edges_ref[1, exposure - 1, layer, tile] = kept[rows - REACH :]


def keep(psi, phi, mask):
    exposures, rows, cols = psi.shape
    tiles = cols // LANES
    later = exposures - 1
    f32 = jnp.float32
    return pl.pallas_call(
        keep_kernel,
        out_shape=(
            jax.ShapeDtypeStruct((2, later, 2, tiles, REACH, LANES), f32),
            jax.ShapeDtypeStruct((later, 2, tiles, rows - 2 * REACH, LANES), f32),
            jax.ShapeDtypeStruct((2, tiles, rows, LANES), f32),
        ),
        compiler_params=pltpu.CompilerParams(vmem_limit_bytes=32 * MIB),
    )(psi, phi, mask)


def stack_kernel(pieces, tiles, later, rows, per_device, *refs):
    velocity_ref, offset_ref, owner_ref = refs[:3]
    piece_refs = refs[3 : 3 + 5 * pieces]
    out_ref, image, first, sems = refs[3 + 5 * pieces :]
    all_tiles = pieces * tiles
    step = pl.program_id(0)
    lane = lax.broadcasted_iota(jnp.int32, (8, LANES), 1)

    @pl.when(step == 0)
    def _():
        waves = [[] for _ in range(later + 1)]
        started = 0
        for exposure in range(later):
            for piece in range(pieces):
                above, edges, mid, below, _ = piece_refs[5 * piece : 5 * piece + 5]
                place = owner_ref[piece] * tiles
                moves = (
                    (above.at[exposure], 0, REACH),
                    (edges.at[0, exposure], REACH, REACH),
                    (mid.at[exposure], 2 * REACH, rows - 2 * REACH),
                    (edges.at[1, exposure], rows, REACH),
                    (below.at[exposure], rows + REACH, REACH),
                )
                for source, start, count in moves:
                    target = image.at[exposure, :, 0, pl.ds(1 + place, tiles), pl.ds(start, count), :]
                    waves[exposure].append(pltpu.make_async_copy(source, target, sems.at[started]))
                    started += 1
        for piece in range(pieces):
            target = first.at[:, pl.ds(owner_ref[piece] * tiles, tiles)]
            source = piece_refs[5 * piece + 4]
            waves[later].append(pltpu.make_async_copy(source, target, sems.at[started]))
            started += 1
        for wave in waves:
            for copy in wave:
                copy.start()
        depth = image.shape[4]
        blank = jnp.zeros((depth, LANES), jnp.float32)
        for exposure in range(later):
            for layer in range(2):
                image[exposure, layer, 0, 0] = blank
                for part in range(4):
                    image[exposure, layer, part, all_tiles + 1] = blank
                for tile in range(all_tiles):
                    image[exposure, layer, 0, tile + 1, rows + 2 * REACH :] = blank[rows + 2 * REACH :]
        groups = depth // 8

        def interpolate(exposure, index, carry):
            layer = index // groups
            here = pl.ds(pl.multiple_of(index % groups * 8, 8), 8)
            values = [image[exposure, layer, 0, tile, here, :] for tile in range(all_tiles + 2)]
            moved = [pltpu.roll(value, LANES - 1, 1) for value in values]
            for tile in range(all_tiles + 1):
                slope = jnp.where(lane < LANES - 1, moved[tile], moved[tile + 1]) - values[tile]
                for part in range(1, 4):
                    image[exposure, layer, part, tile, here, :] = values[tile] + (0.25 * part) * slope
            return carry

        for exposure in range(later):
            for copy in waves[exposure]:
                copy.wait()
            lax.fori_loop(0, 2 * groups, functools.partial(interpolate, exposure), 0)
        for copy in waves[later]:
            copy.wait()

    index = owner_ref[0] * per_device + step
    plans = []
    for exposure in range(later):
        row_shift = velocity_ref[index, 0] * offset_ref[exposure + 1]
        col_shift = velocity_ref[index, 1] * offset_ref[exposure + 1]
        frac_row = jnp.broadcast_to((row_shift & 3).astype(jnp.float32) * 0.25, (8, LANES))
        start = LANES + (col_shift >> 2)
        inside = start & (LANES - 1)
        plans.append(
            (
                REACH + (row_shift >> 2),
                frac_row,
                col_shift & 3,
                start >> 7,
                (LANES - inside) & (LANES - 1),
                lane < LANES - inside,
            )
        )

    def row_group(group, carry):
        def turned(exposure, layer, tile):
            base, frac_row, part, skip, turn, _ = plans[exposure]
            upper = image[exposure, layer, part, skip + tile, pl.ds(base + 8 * group, 8), :]
            lower = image[exposure, layer, part, skip + tile, pl.ds(base + 8 * group + 1, 8), :]
            return pltpu.roll(upper + frac_row * (lower - upper), turn, 1)

        lanes = [(e, l) for e in range(later) for l in range(2)]
        held = {key: turned(*key, 0) for key in lanes}
        done = []
        for tile in range(all_tiles):
            total = [first[layer, tile, pl.ds(pl.multiple_of(8 * group, 8), 8), :] for layer in range(2)]
            for key in lanes:
                following = turned(*key, tile + 1)
                total[key[1]] += jnp.where(plans[key[0]][5], held[key], following)
                held[key] = following
            done.append(total[0] * lax.rsqrt(jnp.maximum(total[1], 1.0)))
        for tile in range(all_tiles):
            out_ref[0, group, tile] = done[tile]
        return carry

    lax.fori_loop(0, rows // 8, row_group, 0)


def stack(velocities, time_offsets, owners, pieces, per_device):
    count = len(pieces)
    later, _, tiles, _, _ = pieces[0][2].shape
    rows = pieces[0][4].shape[2]
    all_tiles = count * tiles
    depth = rows + 2 * REACH + 8
    smem = pl.BlockSpec(memory_space=pltpu.SMEM)
    anywhere = pl.BlockSpec(memory_space=pl.ANY)
    flat = [array for piece in pieces for array in piece]
    out = pl.pallas_call(
        functools.partial(stack_kernel, count, tiles, later, rows, per_device),
        grid=(per_device,),
        out_shape=jax.ShapeDtypeStruct((per_device, rows // 8, all_tiles, 8, LANES), jnp.float32),
        in_specs=[smem] * 3 + [anywhere] * len(flat),
        out_specs=pl.BlockSpec((1, rows // 8, all_tiles, 8, LANES), lambda v: (v, 0, 0, 0, 0)),
        scratch_shapes=[
            pltpu.VMEM((later, 2, 4, all_tiles + 2, depth, LANES), jnp.float32),
            pltpu.VMEM((2, all_tiles, rows, LANES), jnp.float32),
            pltpu.SemaphoreType.DMA(((5 * later + 1) * count,)),
        ],
        compiler_params=pltpu.CompilerParams(vmem_limit_bytes=56 * MIB),
    )(velocities, time_offsets, owners, *flat)
    return out.transpose(0, 1, 3, 2, 4).reshape(per_device, rows, all_tiles * LANES)


def after(value, *earlier):
    return lax.optimization_barrier((value, *earlier))[0]


def body(psi, phi, mask, velocities, time_offsets):
    count = lax.axis_size("vel")
    skies = lax.axis_size("sky")
    per_device = velocities.shape[0] // count
    me = lax.axis_index("vel")
    edges, mid, first = keep(psi, phi, mask)

    def swap(value, bits):
        return lax.ppermute(value, "vel", [(i, i ^ bits) for i in range(count)])

    def from_rows_above(value):
        return lax.ppermute(value, "sky", [(i, i + 1) for i in range(skies - 1)])

    def from_rows_below(value):
        return lax.ppermute(value, "sky", [(i + 1, i) for i in range(skies - 1)])

    far = [2 * k for k in range(1, count // 2)]
    above, below = from_rows_above(edges[1]), from_rows_below(edges[0])
    far_edges = [edges] + [swap(edges, bits) for bits in far]
    far_mid = [mid] + [swap(mid, bits) for bits in far]
    sent = after(first, far_edges[-1], above, below)
    far_first = [first] + [swap(sent, bits) for bits in far]
    above, below = [above], [below]
    for value in far_edges[1:]:
        above.append(from_rows_above(value[1]))
        below.append(from_rows_below(value[0]))
    far_mid = [mid] + [after(value, above[-1], below[-1]) for value in far_mid[1:]]
    pieces, owners = [], []
    for k in range(count // 2):
        pieces.append((above[k], far_edges[k], far_mid[k], below[k], far_first[k]))
        owners.append(me ^ (2 * k))
    for k in range(count // 2):
        pieces.append(tuple(swap(array, 1) for array in pieces[k]))
        owners.append(me ^ (2 * k + 1))
    owners = jnp.stack(owners).astype(jnp.int32)
    return stack(velocities, time_offsets, owners, pieces, per_device)


def solution(mesh):
    return jax.shard_map(
        body,
        mesh=mesh,
        in_specs=(P(None, "sky", "vel"), P(None, "sky", "vel"), P(None, "sky", "vel"), P(), P()),
        out_specs=P("vel", "sky", None),
        check_vma=False,
    )
```
